128 devices in a mesh: ctx: 8 (over z_hi, y), tp: 16 (over z_lo, x, core).
Axes of the slice: x: 4, y: 4, z: 4 (z_hi: 2, z_lo: 2; z = z_hi * 2 + z_lo), core: 2. Of those that a mesh axis runs over, the one named last changes fastest.
Arguments:
- out_grad: bfloat16 [16384, 4096], P(('ctx', 'tp')), may hold values from -6 to 6
- combine_weights: bfloat16 [16384, 8], P(('ctx', 'tp')), may hold values from 0.029907227 to 0.3984375
- expert_ids: int32 [16384, 8], P(('ctx', 'tp')), may hold values from 0 to 127, all different within a row; in each aligned block of 128 rows (0 to 127, 128 to 255, ...) at most 10 rows name the same one
- hidden_saved: bfloat16 [128, 1280, 1536], P(('ctx', 'tp')), may hold values from -0.29882812 to 0.29882812
- down_weight: bfloat16 [128, 1536, 4096], P(('ctx', 'tp')), may hold values from -0.15625 to 0.15625
Outputs:
- hidden_grad: bfloat16 [128, 1280, 1536], P(('ctx', 'tp'))
- combine_grad: float32 [16384, 8], P(('ctx', 'tp'))
The draws below stay inside these ranges and needn't reach their ends.
Inputs may be any that keep to these rules, and one draw needn't show every extreme that they name: `expert_ids`: the 8 ids of a token differ. Among the rows of one device no expert is named more than 10 times, a bound that some block reaches.
All inputs are finite; a program needn't handle non-finite values.
Results may differ from the reference program's by a relative error of at most 0.001.
Values may be sent and summed in bfloat16 or wider, within the bound.
A program may use at most 192 MiB of HBM per device.

```python
import math
import jax
import jax.numpy as jnp
import numpy as np
from jax import lax

D = 4096
FF = 1536
TOPK = 8
TOK_DEV = 128
EXPERTS = 128
TOKENS = 16384
CAP = 10
DEVICES = 128


def shard_levels(rng, shape, split, low, top_value):
    level, own = 1.0, jax.random.fold_in(rng, 6)
    for axis_at, shards_of in split:
        steps = jnp.exp(jax.random.uniform(jax.random.fold_in(own, axis_at), (shards_of,), jnp.float32, low / len(split), top_value / len(split)))
        level = level * jnp.repeat(steps, shape[axis_at] // shards_of).reshape([-1 if axis == axis_at else 1 for axis in range(len(shape))])
    return level


def deal_out(rng, own, number, rows, amount, top, limit, slope):
    ranking = jax.random.permutation(rng, amount)
    heavy_load, usual = shares(amount, rows * top, limit, slope, True), shares(amount, rows * top, limit, slope, False)
    places = jnp.arange(amount)

    def named(tallies, offset_by):
        used = int((tallies > 0).sum())
        fixed = max(1, used // 4)
        moved = fixed + (places - fixed + offset_by * (used - fixed)) % max(1, amount - fixed)
        return jnp.zeros((amount,), jnp.int32).at[ranking[jnp.where(places < fixed, places, moved)]].set(jnp.asarray(tallies, jnp.int32))

    tallies = jnp.where(number % 4 == 0, named(heavy_load, number // 4), named(usual, number - number // 4 - 1))
    mixed = jax.random.permutation(jax.random.fold_in(own, 3), amount)
    donor, sink = mixed[0:amount // 2 * 2:2], mixed[1:amount // 2 * 2:2]
    slack = jnp.minimum(tallies[donor] - 1, limit - tallies[sink]) // 2
    slack = jnp.where((donor == ranking[0]) | (sink == ranking[0]) | (tallies[sink] == 0), 0, jnp.maximum(slack, 0))
    moved = jax.random.randint(jax.random.fold_in(own, 4), (amount // 2,), 0, 1 << 20) % (slack + 1)
    tallies = tallies.at[donor].add(-moved).at[sink].add(moved)
    labels = jnp.searchsorted(jnp.cumsum(tallies), jnp.arange(rows * top), side="right").astype(jnp.int32)
    table = labels.reshape(top, rows).T
    table = table[jax.random.permutation(jax.random.fold_in(own, 1), rows)]
    offset_by = jax.random.randint(jax.random.fold_in(own, 2), (rows, 1), 0, top)
    return jnp.take_along_axis(table, (jnp.arange(top)[None, :] + offset_by) % top, axis=1)


def shares(number_of, total, reach, slope, full):
    loads = [(1 << 20) // math.isqrt(grade ** slope) + 1 for grade in range(1, number_of + 1)]
    largest = reach if full else min(reach, max(-(-total // number_of), total * loads[0] // sum(loads)))
    least = 1 if total - largest >= number_of - 1 else 0
    given, spare = [largest] + [least] * (number_of - 1), total - largest - least * (number_of - 1)
    while spare > 0:
        movable = [i for i in range(1, number_of) if given[i] < largest] or [i for i in range(1, number_of) if given[i] < reach]
        pool, remaining = sum([loads[i] for i in movable]), spare
        for i in movable:
            addition = min(reach - given[i], max(1, remaining * loads[i] // pool), spare)
            given[i] = given[i] + addition
            spare = spare - addition
    return np.array(given)


def gaussian(own_key, extent, scale, limit, cuts=(), kind=jnp.bfloat16):
    entries = scale * jax.random.normal(own_key, extent, jnp.float32)
    if cuts:
        entries = entries * shard_levels(own_key, extent, cuts, -0.22, 0.18)
    return jnp.clip(entries, -limit, limit).astype(kind)


def setup_inputs(seed: int = 0) -> dict:
    seeds = jax.random.split(jax.random.key(seed), 6)
    out_grad = gaussian(seeds[0], (TOKENS, D), 1.0, 6.0, ((0, 128),))
    combine_weights = jnp.clip(0.029907227 + 0.36853027 * jax.random.uniform(seeds[1], (TOKENS, TOPK), jnp.float32) ** shard_levels(seeds[1], (TOKENS, TOPK), ((0, 128),), -0.2, 0.2), 0.029907227, 0.3984375).astype(jnp.bfloat16)
    expert_ids_keys = jax.random.split(jax.random.fold_in(seeds[2], 1), TOKENS // TOK_DEV)
    expert_ids_turns = jax.random.permutation(jax.random.fold_in(seeds[2], 3), TOKENS // TOK_DEV)
    expert_ids = jax.vmap(lambda own, number: deal_out(jax.random.fold_in(seeds[2], 2), own, number, TOK_DEV, EXPERTS, TOPK, CAP, 2))(expert_ids_keys, expert_ids_turns).reshape((TOKENS, TOPK))
    hidden_saved = gaussian(seeds[3], (EXPERTS, DEVICES * CAP, FF), 0.05, 0.29882812, ((0, 128),))
    down_weight = gaussian(seeds[4], (EXPERTS, FF, D), FF ** -0.5, 0.15625, ((0, 128),))
    return {"out_grad": out_grad, "combine_weights": combine_weights, "expert_ids": expert_ids, "hidden_saved": hidden_saved, "down_weight": down_weight}


def reference(out_grad, combine_weights, expert_ids, hidden_saved, down_weight):
    total = DEVICES * CAP
    blocks = expert_ids.reshape(DEVICES, TOK_DEV * TOPK).astype(jnp.int32)
    onehot = (blocks[:, :, None] == jnp.arange(EXPERTS, dtype=jnp.int32)[None, None, :]).astype(jnp.int32)
    position = jnp.sum(jnp.cumsum(onehot, axis=1) * onehot, axis=2) - 1
    source = jnp.arange(DEVICES, dtype=jnp.int32)[:, None]
    slot_index = (blocks * total + source * CAP + position).reshape(-1).astype(jnp.int32)
    token_index = (jnp.arange(TOKENS * TOPK, dtype=jnp.int32) // TOPK).astype(jnp.int32)
    table = jnp.full((EXPERTS * total,), -1, jnp.int32).at[slot_index].set(token_index)
    scales = jnp.zeros((EXPERTS * total,), jnp.float32).at[slot_index].set(
        combine_weights.reshape(-1).astype(jnp.float32))
    table = table.reshape(EXPERTS, total)
    scales = scales.reshape(EXPERTS, total)

    def expert(packed):
        index, scale, saved, weight = packed
        picked = out_grad[jnp.maximum(index, 0)]
        rows_in = jnp.where((index >= 0)[:, None], picked, jnp.zeros((), jnp.bfloat16))
        raw = jnp.dot(rows_in, weight.T, preferred_element_type=jnp.float32)
        grad = (scale[:, None] * raw).astype(jnp.bfloat16)
        back = jnp.sum(saved.astype(jnp.float32) * raw, axis=1)
        return grad, back

    hidden_grad, backs = lax.map(expert, (table, scales, hidden_saved, down_weight))
    combine_grad = backs.reshape(-1)[slot_index].reshape(TOKENS, TOPK)
    return hidden_grad, combine_grad
```

```python
import jax
import jax.numpy as jnp
from jax import lax
from jax.experimental import pallas as pl
from jax.experimental.pallas import tpu as pltpu
from jax.sharding import PartitionSpec as P

MESH = pl.DeviceIdType.MESH
F32 = jnp.float32
BF16 = jnp.bfloat16
CAP = 10
PARTS = (0, 1, 2)


def place(z, y, x, c):
    return ((z // 2) * 4 + y, (z % 2) * 8 + x * 2 + c)


def number(z, y, x, c):
    return (z // 2) * 64 + y * 16 + (z % 2) * 8 + x * 2 + c


def iota(shape, dim):
    return lax.broadcasted_iota(jnp.int32, shape, dim)


def div(a, b):
    return lax.div(a, jnp.int32(b))


def rem(a, b):
    return lax.rem(a, jnp.int32(b))


def dot(a, b):
    return lax.dot_general(a, b, (((1,), (0,)), ((), ())), preferred_element_type=F32)


def dot_t(a, b):
    return lax.dot_general(a, b, (((1,), (1,)), ((), ())), preferred_element_type=F32)


def kernel(
    halves, starts, ff,
    table_ref, grad_ref, saved_ref, weight_ref,
    out_ref, comb_ref,
    ag0, ag1, ag2, ids, pos, snd0, snd1, snd2, rcv0, rcv1, rcv2, y0, y1, y2,
    perm, wv, raw, hs, cws, cwr, sbs, sbr,
    s_ag, r_ag, s_id, r_id, s_mv, r_mv, s_cw, r_cw, s_sb, r_sb, l_w, l_hs, l_out, l_own,
):
    ag, snd, rcv, yb = (ag0, ag1, ag2), (snd0, snd1, snd2), (rcv0, rcv1, rcv2), (y0, y1, y2)
    ctx, tp = lax.axis_index("ctx"), lax.axis_index("tp")
    z, y, x, c = (ctx // 4) * 2 + tp // 8, ctx % 4, (tp // 2) % 4, tp % 2
    me = ctx * 16 + tp
    at = (z, y, x)

    def mate(p, d):
        return place(*(((v + d) % 4 if q == p else v) for q, v in enumerate((z, y, x))), c)

    def other(i):
        return place((z + i // 32) % 4, (y + (i // 8) % 4) % 4, (x + (i // 2) % 4) % 4, (c + i % 2) % 2)

    barrier = pltpu.get_barrier_semaphore()

    def greet(i, _):
        pl.semaphore_signal(barrier, inc=1, device_id=other(i), device_id_type=MESH)
        return 0

    lax.fori_loop(1, 128, greet, 0)

    own = []
    for p in PARTS:
        cols = pl.ds(starts[p], 2 * halves[p])
        own.append(pltpu.make_async_copy(grad_ref.at[:, cols], ag[p].at[at[p]], l_own.at[p]))
        own[-1].start()
    load_w = pltpu.make_async_copy(weight_ref.at[0], wv, l_w)
    load_w.start()
    load_hs = pltpu.make_async_copy(saved_ref.at[0], hs, l_hs)
    load_hs.start()
    for p in PARTS:
        ids[p, at[p]] = table_ref[:8, :]

    for q in range(2):
        row = iota((640, 1), 0)
        chunk, b, g, j = div(row, 320), rem(div(row, 80), 4), rem(div(row, 10), 8), rem(row, 10)
        if q == 0:
            source = g * 80 + chunk * 40 + b * 10 + j
        else:
            source = (b * 2 + rem(g, 2)) * 80 + chunk * 40 + div(g, 2) * 10 + j
        perm[q] = jnp.where(iota((640, 640), 1) == source, 1.0, 0.0).astype(BF16)

    before = jnp.where(iota((128, 128), 0) < iota((128, 128), 1), 1.0, 0.0).astype(BF16)
    expert = iota((128, 128), 0).astype(F32)

    def positions(table):
        named = jnp.zeros((128, 128), F32)
        for k in range(8):
            named = named + jnp.where(expert == table[k : k + 1, :], 1.0, 0.0)
        earlier = dot(named.astype(BF16), before)
        return jnp.where(named > 0.0, earlier, -1.0)

    table = table_ref[...]
    mine = positions(table[:8, :])
    scale = jnp.zeros((128, 128), F32)
    for k in range(8):
        scale = scale + jnp.where(expert == table[k : k + 1, :], table[8 + k : 9 + k, :], 0.0)
    lane = iota((128, 128), 1)
    rows = jnp.zeros((128, 128), F32)
    for j in range(CAP):
        column = jnp.sum(jnp.where(mine == float(j), scale, 0.0), axis=1, keepdims=True)
        rows = rows + jnp.where(lane == j, column, 0.0)
    cws[...] = rows.reshape(128, 1, 128)

    pl.semaphore_wait(barrier, 127)

    def gather(p, d):
        cols = pl.ds(starts[p], 2 * halves[p])
        return pltpu.make_async_remote_copy(
            grad_ref.at[:, cols], ag[p].at[at[p]], s_ag.at[p, d], r_ag.at[p, at[p]],
            device_id=mate(p, d), device_id_type=MESH,
        )

    def gather_ids(p, d):
        return pltpu.make_async_remote_copy(
            table_ref.at[pl.ds(0, 8)], ids.at[p, at[p]], s_id.at[p, d], r_id.at[p, at[p]],
            device_id=mate(p, d), device_id_type=MESH,
        )

    for d in (1, 3, 2):
        for p in PARTS:
            gather_ids(p, d).start()
    for d in (1, 3, 2):
        for p in PARTS:
            gather(p, d).start()

    def send_cw(i):
        d = other(i)
        return pltpu.make_async_remote_copy(
            cws.at[d[0] * 16 + d[1]], cwr.at[me], s_cw, r_cw, device_id=d, device_id_type=MESH
        )

    lax.fori_loop(1, 128, lambda i, _: (send_cw(i).start(), 0)[1], 0)
    cwr[me] = cws[me]

    for p in PARTS:
        for d in (1, 2, 3):
            b = (at[p] + d) % 4
            pltpu.make_async_remote_copy(
                table_ref.at[pl.ds(0, 8)], ids.at[p, b], s_id.at[p, d], r_id.at[p, b],
                device_id=mate(p, d), device_id_type=MESH,
            ).wait_recv()
    for p in PARTS:
        for b in range(4):
            pos[p, :, b * 128 : (b + 1) * 128] = positions(ids[p, b]).astype(BF16)

    raw[...] = jnp.zeros_like(raw)

    for p in PARTS:
        own[p].wait()
    for d in (1, 3, 2):
        for p in PARTS:
            b = (at[p] + d) % 4
            cols = pl.ds(starts[p], 2 * halves[p])
            pltpu.make_async_remote_copy(
                grad_ref.at[:, cols], ag[p].at[b], s_ag.at[p, d], r_ag.at[p, b],
                device_id=mate(p, d), device_id_type=MESH,
            ).wait_recv()

    slot = (y * 8 + x * 2 + c, z * 8 + x * 2 + c, y * 8 + z * 2 + c)

    def target(p, k, g):
        d = (k + 1) % 4
        if p == 0:
            return (z, (y + d) % 4, g // 2, g % 2)
        if p == 1:
            return ((z + d) % 4, y, g // 2, g % 2)
        return (g // 2, (y + d) % 4, x, g % 2)

    def move(p, k, g):
        return pltpu.make_async_remote_copy(
            snd[p].at[k * 8 + g], rcv[p].at[slot[p]], s_mv.at[p, k * 8 + g], r_mv.at[p, slot[p]],
            device_id=place(*target(p, k, g)), device_id_type=MESH,
        )

    def keep(p, g):
        return pltpu.make_async_copy(snd[p].at[24 + g], rcv[p].at[slot[p]], r_mv.at[p, slot[p]])

    def pick(k, p):
        row = iota((320, 1), 0)
        e, b, j = div(row, 40), rem(div(row, 10), 4), rem(row, 10)
        if p == 2:
            who = number(div(e, 2), target(p, k, 0)[1], x, rem(e, 2))
        else:
            first = target(p, k, 0)
            who = number(first[0], first[1], 0, 0) + e
        chosen = jnp.where(iota((320, 128), 1) == who, 1.0, 0.0).astype(BF16)
        value = dot(chosen, pos[p])
        hit = (value == j.astype(F32)) & (div(iota((1, 512), 1), 128) == b)
        onehot = jnp.where(hit, 1.0, 0.0).astype(BF16)
        h = halves[p]
        parts = [dot(onehot, ag[p][:, :, i * h : (i + 1) * h].reshape(512, h)) for i in range(2)]
        for g in range(8):
            both = [part[g * 40 : g * 40 + 40] for part in parts]
            snd[p][k * 8 + g] = jnp.concatenate(both, axis=0).astype(BF16)

    def send_stage(k, _):
        for p in PARTS:
            pick(k, p)

        def send(i, _):
            for p in PARTS:
                a = (z if p == 2 else x) + i + 1 + k
                g = (a % 4) * 2 + (c + i // 4) % 2

                if p == 2:
                    itself = (k == 3) & (g == z * 2 + c)
                else:
                    itself = (k == 3) & (g == x * 2 + c)

                @pl.when(itself)
                def _():
                    keep(p, g).start()

                @pl.when(jnp.logical_not(itself))
                def _():
                    move(p, k, g).start()
            return 0

        return lax.fori_loop(0, 8, send, 0)

    lax.fori_loop(0, 4, send_stage, 0)

    load_w.wait()
    load_hs.wait()
    pltpu.make_async_remote_copy(
        cws.at[pl.ds(0, 127)], cwr.at[pl.ds(0, 127)], s_cw, r_cw, device_id=other(1), device_id_type=MESH
    ).wait_recv()

    def arrive(p, k):
        d = (k + 1) % 4
        block = ((y + 4 - d) % 4, (z + 4 - d) % 4, (y + 4 - d) % 4)[p]

        def wait(g, _):
            i = block * 8 + g
            pltpu.make_async_copy(snd[p].at[0], rcv[p].at[i], r_mv.at[p, i]).wait()
            return 0

        lax.fori_loop(0, 8, wait, 0)
        h = halves[p]
        got = rcv[p][pl.ds(block * 8, 8)].reshape(640, h)
        yb[p][...] = dot(perm[1 if p == 2 else 0], got).astype(BF16)
        return block

    step = 512

    def back(unit_y, unit_z):
        first = number(unit_z, unit_y, 0, 0)
        here = pl.ds(pl.multiple_of((unit_y * 4 + unit_z) * 80, 80), 80)
        there = pl.ds(pl.multiple_of(first * CAP, 80), 80)
        row = iota((80, 1), 0)
        j = rem(row, 10)
        lanes = iota((80, 128), 1)
        spread = jnp.where(iota((80, 8), 1) == div(row, 10), 1.0, 0.0)
        weights = dot(spread.astype(BF16), cwr[pl.ds(first, 8)].reshape(8, 128).astype(BF16))
        weight = jnp.sum(jnp.where(lanes == j, weights, 0.0), axis=1, keepdims=True)
        total = raw[here, :]
        summed = jnp.sum(hs[there, :].astype(F32) * total, axis=1, keepdims=True)
        hs[there, :] = (weight * total).astype(BF16)
        pltpu.make_async_copy(hs.at[there], out_ref.at[0, there], l_out.at[unit_y * 4 + unit_z]).start()
        cells = jnp.where(lanes == j, summed, 0.0)
        for g in range(8):
            line = jnp.sum(cells[g * 10 : g * 10 + 10, :], axis=0, keepdims=True)
            sbs[first + g] = line

            @pl.when(first + g == me)
            def _():
                sbr[me] = line

            @pl.when(first + g != me)
            def _():
                pltpu.make_async_remote_copy(
                    sbs.at[first + g], sbr.at[me], s_sb, r_sb,
                    device_id=place(unit_z, unit_y, g // 2, g % 2), device_id_type=MESH,
                ).start()

    def receive_stage(k, _):
        y_block = arrive(0, k)
        arrive(2, k)
        here = pl.ds(pl.multiple_of(y_block * 320, 320), 320)

        def multiply(n, _):
            out = pl.ds(pl.multiple_of(n * step, step), step)
            acc = jnp.zeros((320, step), F32)
            for p in (0, 2):
                h = halves[p]
                for i in range(2):
                    w = wv[out, starts[p] + i * h : starts[p] + (i + 1) * h]
                    acc = acc + dot_t(yb[p][i * 320 : (i + 1) * 320, :], w)
            raw[here, out] += acc
            return 0

        lax.fori_loop(0, ff // step, multiply, 0)
        z_block = arrive(1, k)

        def multiply_y(n, _):
            out = pl.ds(pl.multiple_of(n * step, step), step)
            acc = jnp.zeros((320, step), F32)
            h = halves[1]
            for i in range(2):
                w = wv[out, starts[1] + i * h : starts[1] + (i + 1) * h]
                acc = acc + dot_t(yb[1][i * 320 : (i + 1) * 320, :], w)
            for b in range(4):
                rows_b = pl.ds(pl.multiple_of(b * 320 + z_block * 80, 80), 80)
                raw[rows_b, out] += acc[b * 80 : (b + 1) * 80]
            return 0

        lax.fori_loop(0, ff // step, multiply_y, 0)

        def finish(i, _):
            back(y_block, (z + 4 - (i + 1) % 4) % 4)
            return 0

        lax.fori_loop(0, k + 1, finish, 0)

        def finish_z(i, _):
            back((y + 4 - (i + 1) % 4) % 4, z_block)
            return 0

        lax.fori_loop(0, k, finish_z, 0)
        return 0

    lax.fori_loop(0, 4, receive_stage, 0)

    pltpu.make_async_remote_copy(
        sbs.at[pl.ds(0, 127)], sbr.at[pl.ds(0, 127)], s_sb, r_sb, device_id=other(1), device_id_type=MESH
    ).wait_recv()
    returned = sbr[...].reshape(128, 128)
    found = jnp.zeros((128, 128), F32)
    for j in range(CAP):
        found = found + jnp.where(mine == float(j), returned[:, j : j + 1], 0.0)
    for k in range(8):
        chosen = jnp.where(expert == table[k : k + 1, :], found, 0.0)
        comb_ref[k : k + 1, :] = jnp.sum(chosen, axis=0, keepdims=True)

    for d in (1, 3, 2):
        for p in PARTS:
            gather(p, d).wait_send()
            gather_ids(p, d).wait_send()
    pltpu.make_async_remote_copy(
        cws.at[pl.ds(0, 127)], cwr.at[pl.ds(0, 127)], s_cw, r_cw, device_id=other(1), device_id_type=MESH
    ).wait_send()
    pltpu.make_async_remote_copy(
        sbs.at[pl.ds(0, 127)], sbr.at[pl.ds(0, 127)], s_sb, r_sb, device_id=other(1), device_id_type=MESH
    ).wait_send()

    def sent(i, _):
        for p in PARTS:
            g = i % 8
            itself = (i // 8 == 3) & (g == (z if p == 2 else x) * 2 + c)

            @pl.when(jnp.logical_not(itself))
            def _():
                move(p, i // 8, g).wait_send()
        return 0

    lax.fori_loop(0, 32, sent, 0)

    def stored(u, _):
        pltpu.make_async_copy(hs.at[pl.ds(0, 80)], out_ref.at[0, pl.ds(0, 80)], l_out.at[u]).wait()
        return 0

    lax.fori_loop(0, 16, stored, 0)


def per_device(out_grad, combine_weights, expert_ids, hidden_saved, down_weight):
    slots, ff = hidden_saved.shape[1:]
    units = out_grad.shape[1] // 256
    counts = [(units + i) // 3 for i in range(3)]
    halves = tuple(128 * n for n in counts)
    starts = (0, 2 * halves[0], 2 * (halves[0] + halves[1]))
    table = jnp.concatenate([expert_ids.T.astype(F32), combine_weights.T.astype(F32)], axis=0)
    anywhere = pl.BlockSpec(memory_space=pl.ANY)
    vmem = pl.BlockSpec(memory_space=pltpu.VMEM)
    dma = pltpu.SemaphoreType.DMA

    def body(*refs):
        kernel(halves, starts, ff, *refs)

    hidden_grad, combine = pl.pallas_call(
        body,
        out_shape=(
            jax.ShapeDtypeStruct(hidden_saved.shape, BF16),
            jax.ShapeDtypeStruct((8, 128), F32),
        ),
        in_specs=[vmem, anywhere, anywhere, anywhere],
        out_specs=(anywhere, vmem),
        scratch_shapes=[pltpu.VMEM((4, 128, 2 * h), BF16) for h in halves]
        + [pltpu.VMEM((3, 4, 8, 128), F32), pltpu.VMEM((3, 128, 512), BF16)]
        + [pltpu.VMEM((32, 80, h), BF16) for h in halves] * 2
        + [pltpu.VMEM((640, h), BF16) for h in halves]
        + [
            pltpu.VMEM((2, 640, 640), BF16),
            pltpu.VMEM((ff, out_grad.shape[1]), BF16),
            pltpu.VMEM((slots, ff), F32),
            pltpu.VMEM((slots, ff), BF16),
        ]
        + [pltpu.VMEM((128, 1, 128), F32)] * 4
        + [dma((3, 4))] * 4
        + [dma((3, 32))] * 2
        + [dma] * 6
        + [dma((16,)), dma((3,))],
        compiler_params=pltpu.CompilerParams(
            collective_id=0, has_side_effects=True, vmem_limit_bytes=62 << 20
        ),
    )(table, out_grad, hidden_saved, down_weight)
    return hidden_grad, combine.T


def solution(mesh):
    both = ("ctx", "tp")
    in_specs = (P(both, None), P(both, None), P(both, None), P(both, None, None), P(both, None, None))
    out_specs = (P(both, None, None), P(both, None))
    return jax.shard_map(
        per_device, mesh=mesh, in_specs=in_specs, out_specs=out_specs, check_vma=False
    )
```

```python
import jax
import jax.numpy as jnp
from jax import lax
from jax.experimental import pallas as pl
from jax.experimental.pallas import tpu as pltpu
from jax.sharding import PartitionSpec as P

MESH = pl.DeviceIdType.MESH
F32 = jnp.float32
BF16 = jnp.bfloat16
CAP = 10
AXES = (0, 1, 2)
SETS = (0, 1, 2)
SHARES = ((2, 2, 2), (2, 2, 2), (1, 1, 2))


def place(z, y, x, c):
    return ((z // 2) * 4 + y, (z % 2) * 8 + x * 2 + c)


def number(z, y, x, c):
    return (z // 2) * 64 + y * 16 + (z % 2) * 8 + x * 2 + c


def iota(shape, dim):
    return lax.broadcasted_iota(jnp.int32, shape, dim)


def div(a, b):
    return lax.div(a, jnp.int32(b))


def rem(a, b):
    return lax.rem(a, jnp.int32(b))


def dot(a, b):
    return lax.dot_general(a, b, (((1,), (0,)), ((), ())), preferred_element_type=F32)


def dot_t(a, b):
    return lax.dot_general(a, b, (((1,), (1,)), ((), ())), preferred_element_type=F32)


def kernel(halves, starts, ff, ids_ref, scale_ref, grad_ref, saved_ref, weight_ref, out_ref, comb_ref, *scratch):
    scratch = list(scratch)

    def take(n):
        got = scratch[:n]
        del scratch[:n]
        return got

    ag, snd, rcv = ([take(3) for _ in SETS] for _ in range(3))
    yb = take(3)
    ids, pos, zpos, perm, wv, raw, hs, cws, cwr, sbs, sbr = take(11)
    s_ag, r_ag, s_id, r_id, s_mv, r_mv, s_cw, r_cw, s_sb, r_sb, l_w, l_hs, l_out, l_own = take(14)

    ctx, tp = lax.axis_index("ctx"), lax.axis_index("tp")
    z, y, x, c = (ctx // 4) * 2 + tp // 8, ctx % 4, (tp // 2) % 4, tp % 2
    me = ctx * 16 + tp
    at = (z, y, x)
    slot = (y * 8 + x * 2 + c, z * 8 + x * 2 + c, y * 8 + z * 2 + c)

    def mate(p, d, core):
        return place(*(((v + d) % 4 if q == p else v) for q, v in enumerate(at)), core)

    barrier = pltpu.get_barrier_semaphore()
    for d in (1, 3, 2):
        for p in AXES:
            for core in (c, 1 - c):
                pl.semaphore_signal(barrier, inc=1, device_id=mate(p, d, core), device_id_type=MESH)
    pl.semaphore_signal(barrier, inc=1, device_id=place(z, y, x, 1 - c), device_id_type=MESH)

    own = []
    for s in SETS:
        for p in AXES:
            cols = pl.ds(starts[s][p], 2 * halves[s][p])
            own.append(pltpu.make_async_copy(grad_ref.at[:, cols], ag[s][p].at[at[p]], l_own.at[s * 3 + p]))
            own[-1].start()
    load_w = pltpu.make_async_copy(weight_ref.at[0], wv, l_w)
    load_hs = pltpu.make_async_copy(saved_ref.at[0], hs, l_hs)

    ids_t = ids_ref[...].astype(F32)
    scale_t = scale_ref[...].astype(F32)
    for p in AXES:
        ids[p * 4 + at[p], :8, :] = ids_t
        ids[p * 4 + at[p], 8:, :] = scale_t
    for copy in own:
        copy.wait()
    pl.semaphore_wait(barrier, 19)

    def gather(s, p, d):
        here = ag[s][p].at[at[p]]
        return pltpu.make_async_remote_copy(
            here, here, s_ag.at[s * 3 + p, d], r_ag.at[s * 3 + p, d], device_id=mate(p, d, c), device_id_type=MESH
        )

    def forward(s, p, d):
        half = ag[s][p].at[(at[p] + 4 - d) % 4, pl.ds(64 * (d // 2), 64)]
        return pltpu.make_async_remote_copy(
            half, half, s_ag.at[s * 3 + p, d - 1], r_ag.at[s * 3 + p, d - 1],
            device_id=mate(p, d, c), device_id_type=MESH,
        )

    def gather_ids(p, d):
        here = ids.at[p * 4 + at[p]]
        return pltpu.make_async_remote_copy(
            here, here, s_id, r_id, device_id=mate(p, d, c), device_id_type=MESH
        )

    for d in (1, 3, 2):
        for p in AXES:
            gather_ids(p, d).start()
    for s in SETS:
        for d in (1, 3):
            for p in AXES:
                gather(s, p, d).start()
    load_w.start()
    load_hs.start()

    for q in range(2):
        row = iota((640, 1), 0)
        chunk, b, g, j = div(row, 320), rem(div(row, 80), 4), rem(div(row, 10), 8), rem(row, 10)
        if q == 0:
            source = g * 80 + chunk * 40 + b * 10 + j
        else:
            source = (b * 2 + rem(g, 2)) * 80 + chunk * 40 + div(g, 2) * 10 + j
        perm[q] = jnp.where(iota((640, 640), 1) == source, 1.0, 0.0).astype(BF16)
    raw[...] = jnp.zeros_like(raw)

    before = jnp.where(iota((128, 128), 0) < iota((128, 128), 1), 1.0, 0.0).astype(BF16)
    expert = iota((128, 128), 0).astype(F32)

    def positions(table):
        named = jnp.zeros((128, 128), F32)
        for k in range(8):
            named = named + jnp.where(expert == table[k : k + 1, :], 1.0, 0.0)
        earlier = dot(named.astype(BF16), before)
        return jnp.where(named > 0.0, earlier, -1.0)

    nine = ids.at[pl.ds(0, 9)]
    pltpu.make_async_copy(nine, nine, r_id).wait()
    for p in AXES:
        for b in range(4):
            found = positions(ids[p * 4 + b])
            pos[p, :, b * 128 : (b + 1) * 128] = found.astype(BF16)
            if p == 0:
                zpos[b] = found

    lane8 = iota((8, 128), 1)

    def weigh(unit_y, _):
        first = pl.multiple_of(number(z, unit_y, 0, 0), 8)
        named = (iota((8, 128), 0) + first).astype(F32)
        rows = jnp.zeros((8, 128), F32)
        for b in range(4):
            scale = jnp.zeros((8, 128), F32)
            for k in range(8):
                scale = scale + jnp.where(named == ids[b, k : k + 1, :], ids[b, 8 + k : 9 + k, :], 0.0)
            which = zpos[b, pl.ds(first, 8), :]
            for j in range(CAP):
                column = jnp.sum(jnp.where(which == float(j), scale, 0.0), axis=1, keepdims=True)
                rows = rows + jnp.where(lane8 == b * CAP + j, column, 0.0)
        for g in range(8):
            cws[unit_y * 8 + g] = rows[g : g + 1]
        return 0

    lax.fori_loop(0, 4, weigh, 0)

    def relay(s):
        for d in (1, 3):
            for p in AXES:
                gather(s, p, d).wait_recv()
                forward(s, p, d).start()

    def arrived(s):
        for d in (1, 3):
            for p in AXES:
                forward(s, p, d).wait_recv()

    def target(p, k, g):
        d = (k + 1) % 4
        if p == 0:
            return (z, (y + d) % 4, g // 2, g % 2)
        if p == 1:
            return ((z + d) % 4, y, g // 2, g % 2)
        return (g // 2, (y + d) % 4, x, g % 2)

    def move(s, p, k, g):
        return pltpu.make_async_remote_copy(
            snd[s][p].at[k * 8 + g], rcv[s][p].at[slot[p]], s_mv.at[s, p * 4 + k],
            r_mv.at[s, p * 4 + slot[p] // 8],
            device_id=place(*target(p, k, g)), device_id_type=MESH,
        )

    def keep(s, p, g):
        return pltpu.make_async_copy(
            snd[s][p].at[24 + g], rcv[s][p].at[slot[p]], r_mv.at[s, p * 4 + slot[p] // 8]
        )

    def pick(s, k, p):
        row = iota((320, 1), 0)
        e, b, j = div(row, 40), rem(div(row, 10), 4), rem(row, 10)
        first = target(p, k, 0)
        if p == 2:
            who = number(div(e, 2), first[1], x, rem(e, 2))
        else:
            who = number(first[0], first[1], 0, 0) + e
        chosen = jnp.where(iota((320, 128), 1) == who, 1.0, 0.0).astype(BF16)
        value = dot(chosen, pos[p])
        hit = (value == j.astype(F32)) & (div(iota((1, 512), 1), 128) == b)
        onehot = jnp.where(hit, 1.0, 0.0).astype(BF16)
        h = halves[s][p]
        parts = [dot(onehot, ag[s][p][:, :, i * h : (i + 1) * h].reshape(512, h)) for i in range(2)]
        for g in range(8):
            both = [part[g * 40 : g * 40 + 40] for part in parts]
            snd[s][p][k * 8 + g] = jnp.concatenate(both, axis=0).astype(BF16)

    def send_stage(s, k):
        for p in AXES:
            pick(s, k, p)

        def send(i, _):
            for p in AXES:
                own_g = (z if p == 2 else x) * 2 + c
                g = (((z if p == 2 else x) + i + 1 + k) % 4) * 2 + (c + i // 4) % 2
                itself = (k == 3) & (g == own_g)

                @pl.when(itself)
                def _():
                    keep(s, p, g).start()

                @pl.when(jnp.logical_not(itself))
                def _():
                    move(s, p, k, g).start()
            return 0

        lax.fori_loop(0, 8, send, 0)

    def sent(s, k):
        for p in AXES:
            eight, seven = snd[s][p].at[pl.ds(0, 8)], snd[s][p].at[pl.ds(0, 7)]

            @pl.when(k < 3)
            def _():
                pltpu.make_async_copy(eight, eight, s_mv.at[s, p * 4 + k]).wait()

            @pl.when(k == 3)
            def _():
                pltpu.make_async_copy(seven, seven, s_mv.at[s, p * 4 + k]).wait()

    def arrive(s, p, k):
        d = (k + 1) % 4
        block = ((y + 4 - d) % 4, (z + 4 - d) % 4, (y + 4 - d) % 4)[p]
        rows = rcv[s][p].at[pl.ds(block * 8, 8)]
        pltpu.make_async_copy(rows, rows, r_mv.at[s, p * 4 + block]).wait()
        h = halves[s][p]
        got = rcv[s][p][pl.ds(block * 8, 8)].reshape(640, h)
        yb[p][:, :h] = dot(perm[1 if p == 2 else 0], got).astype(BF16)
        return block

    step = 512

    def terms(s, axes, out):
        acc = jnp.zeros((320, step), F32)
        for p in axes:
            h = halves[s][p]
            for i in range(2):
                w = wv[out, starts[s][p] + i * h : starts[s][p] + (i + 1) * h]
                acc = acc + dot_t(yb[p][i * 320 : (i + 1) * 320, :h], w)
        return acc

    def back(unit_y, unit_z):
        first = number(unit_z, unit_y, 0, 0)
        here = pl.ds(pl.multiple_of((unit_y * 4 + unit_z) * 80, 80), 80)
        there = pl.ds(pl.multiple_of(first * CAP, 80), 80)
        row = iota((80, 1), 0)
        j = rem(row, 10)
        lanes = iota((80, 128), 1)
        spread = jnp.where(iota((80, 8), 1) == div(row, 10), 1.0, 0.0)
        weights = dot(spread.astype(BF16), cwr[pl.ds(unit_y * 8, 8)].reshape(8, 128).astype(BF16))
        weight = jnp.sum(jnp.where(lanes == unit_z * CAP + j, weights, 0.0), axis=1, keepdims=True)
        total = raw[here, :]
        summed = jnp.sum(hs[there, :].astype(F32) * total, axis=1, keepdims=True)
        hs[there, :] = (weight * total).astype(BF16)
        pltpu.make_async_copy(hs.at[there], out_ref.at[0, there], l_out.at[unit_y * 4 + unit_z]).start()
        cells = jnp.where(lanes == j, summed, 0.0)
        for g in range(8):
            line = jnp.sum(cells[g * 10 : g * 10 + 10, :], axis=0, keepdims=True)
            sbs[first + g] = line

            @pl.when(first + g == me)
            def _():
                sbr[me] = line

            @pl.when(first + g != me)
            def _():
                pltpu.make_async_remote_copy(
                    sbs.at[first + g], sbr.at[me], s_sb, r_sb,
                    device_id=place(unit_z, unit_y, g // 2, g % 2), device_id_type=MESH,
                ).start()

    def receive_stage(s, k):
        y_block = arrive(s, 0, k)
        arrive(s, 2, k)
        here = pl.ds(pl.multiple_of(y_block * 320, 320), 320)

        def multiply(n, _):
            out = pl.ds(pl.multiple_of(n * step, step), step)
            raw[here, out] += terms(s, (0, 2), out)
            return 0

        lax.fori_loop(0, ff // step, multiply, 0)
        z_block = arrive(s, 1, k)

        def multiply_y(n, _):
            out = pl.ds(pl.multiple_of(n * step, step), step)
            acc = terms(s, (1,), out)
            for b in range(4):
                rows_b = pl.ds(pl.multiple_of(b * 320 + z_block * 80, 80), 80)
                raw[rows_b, out] += acc[b * 80 : (b + 1) * 80]
            return 0

        lax.fori_loop(0, ff // step, multiply_y, 0)
        if s < SETS[-1]:
            return

        def finish(i, _):
            back(y_block, (z + 4 - (i + 1) % 4) % 4)
            return 0

        lax.fori_loop(0, k + 1, finish, 0)

        def finish_z(i, _):
            back((y + 4 - (i + 1) % 4) % 4, z_block)
            return 0

        lax.fori_loop(0, k, finish_z, 0)

    def loop(lower, upper, *steps):
        def run(k, _):
            for do in steps:
                do(k)
            return 0

        lax.fori_loop(lower, upper, run, 0)

    def send_cw(i):
        unit_y, g = (y + i // 8) % 4, (x * 2 + c + i) % 8
        return pltpu.make_async_remote_copy(
            cws.at[unit_y * 8 + g], cwr.at[slot[0]], s_cw, r_cw,
            device_id=place(z, unit_y, g // 2, g % 2), device_id_type=MESH,
        )

    relay(0)
    stages = 4 * len(SETS)
    behind = 2

    def turn(t, _):
        for s in SETS:

            @pl.when(t == s * 4)
            def _():
                arrived(s)

            @pl.when(t // 4 == s)
            def _():
                send_stage(s, t % 4)

            if s > 0:

                @pl.when(t == s - 1)
                def _():
                    relay(s)

        @pl.when(t == behind - 1)
        def _():
            loop(1, 32, lambda i: send_cw(i).start())
            cwr[slot[0]] = cws[slot[0]]
            load_w.wait()
            load_hs.wait()

        u = t - behind
        for s in SETS:
            if s == SETS[-1]:

                @pl.when(u == s * 4)
                def _():
                    pltpu.make_async_copy(all_cw, all_cw, r_cw).wait()

            @pl.when((u >= s * 4) & (u < s * 4 + 4))
            def _():
                sent(s, u - s * 4)
                receive_stage(s, u - s * 4)
        return 0

    all_cw = cwr.at[pl.ds(0, 31)]
    lax.fori_loop(0, stages + behind, turn, 0)

    all_sb = sbr.at[pl.ds(0, 127)]
    pltpu.make_async_copy(all_sb, all_sb, r_sb).wait()
    returned = sbr[...].reshape(128, 128)
    mine = zpos[z]
    found = jnp.zeros((128, 128), F32)
    for j in range(CAP):
        found = found + jnp.where(mine == float(j), returned[:, j : j + 1], 0.0)
    for k in range(8):
        chosen = jnp.where(expert == ids[z, k : k + 1, :], found, 0.0)
        comb_ref[k : k + 1, :] = jnp.sum(chosen, axis=0, keepdims=True)

    for s in SETS:
        for p in AXES:
            for d in (1, 3):
                gather(s, p, d).wait_send()
                forward(s, p, d).wait_send()
    pltpu.make_async_copy(nine, nine, s_id).wait()
    pltpu.make_async_copy(all_cw, all_cw, s_cw).wait()
    pltpu.make_async_copy(all_sb, all_sb, s_sb).wait()

    def stored(u):
        pltpu.make_async_copy(hs.at[pl.ds(0, 80)], out_ref.at[0, pl.ds(0, 80)], l_out.at[u]).wait()

    loop(0, 16, stored)


def per_device(out_grad, combine_weights, expert_ids, hidden_saved, down_weight):
    slots, ff = hidden_saved.shape[1:]
    halves = tuple(tuple(128 * n for n in share) for share in SHARES)
    starts, at = [], 0
    for s in SETS:
        starts.append([])
        for p in AXES:
            starts[s].append(at)
            at += 2 * halves[s][p]
    anywhere = pl.BlockSpec(memory_space=pl.ANY)
    vmem = pl.BlockSpec(memory_space=pltpu.VMEM)
    dma = pltpu.SemaphoreType.DMA
    flat = [h for s in SETS for h in halves[s]]

    def body(*refs):
        kernel(halves, starts, ff, *refs)

    hidden_grad, combine = pl.pallas_call(
        body,
        out_shape=(
            jax.ShapeDtypeStruct(hidden_saved.shape, BF16),
            jax.ShapeDtypeStruct((8, 128), F32),
        ),
        in_specs=[vmem, vmem, anywhere, anywhere, anywhere],
        out_specs=(anywhere, vmem),
        scratch_shapes=[pltpu.VMEM((4, 128, 2 * h), BF16) for h in flat]
        + [pltpu.VMEM((32, 80, h), BF16) for h in flat] * 2
        + [pltpu.VMEM((640, max(halves[s][p] for s in SETS)), BF16) for p in AXES]
        + [
            pltpu.VMEM((12, 16, 128), F32),
            pltpu.VMEM((3, 128, 512), BF16),
            pltpu.VMEM((4, 128, 128), F32),
            pltpu.VMEM((2, 640, 640), BF16),
            pltpu.VMEM((ff, out_grad.shape[1]), BF16),
            pltpu.VMEM((slots, ff), F32),
            pltpu.VMEM((slots, ff), BF16),
            pltpu.VMEM((32, 1, 128), F32),
            pltpu.VMEM((32, 1, 128), F32),
            pltpu.VMEM((128, 1, 128), F32),
            pltpu.VMEM((128, 1, 128), F32),
        ]
        + [dma((9, 4))] * 2
        + [dma] * 2
        + [dma((3, 12))] * 2
        + [dma] * 6
        + [dma((16,)), dma((9,))],
        compiler_params=pltpu.CompilerParams(
            collective_id=0, has_side_effects=True, vmem_limit_bytes=62 << 20
        ),
    )(expert_ids.T, combine_weights.T, out_grad, hidden_saved, down_weight)
    return hidden_grad, combine.T


def solution(mesh):
    both = ("ctx", "tp")
    in_specs = (P(both, None), P(both, None), P(both, None), P(both, None, None), P(both, None, None))
    out_specs = (P(both, None, None), P(both, None))
    return jax.shard_map(
        per_device, mesh=mesh, in_specs=in_specs, out_specs=out_specs, check_vma=False
    )
```

```python
import jax
import jax.numpy as jnp
from jax import lax
from jax.experimental import pallas as pl
from jax.experimental.pallas import tpu as pltpu
from jax.sharding import PartitionSpec as P

MESH = pl.DeviceIdType.MESH
F32 = jnp.float32
BF16 = jnp.bfloat16
CAP = 10
AXES = (0, 1, 2)
SETS = (0, 1, 2)
SHARES = ((2, 2, 2), (2, 2, 2), (1, 1, 2))


def place(z, y, x, c):
    return ((z // 2) * 4 + y, (z % 2) * 8 + x * 2 + c)


def number(z, y, x, c):
    return (z // 2) * 64 + y * 16 + (z % 2) * 8 + x * 2 + c


def iota(shape, dim):
    return lax.broadcasted_iota(jnp.int32, shape, dim)


def div(a, b):
    return lax.div(a, jnp.int32(b))


def rem(a, b):
    return lax.rem(a, jnp.int32(b))


def dot(a, b):
    return lax.dot_general(a, b, (((1,), (0,)), ((), ())), preferred_element_type=F32)


def dot_t(a, b):
    return lax.dot_general(a, b, (((1,), (1,)), ((), ())), preferred_element_type=F32)


def kernel(halves, starts, ff, ids_ref, scale_ref, grad_ref, saved_ref, weight_ref, out_ref, comb_ref, *scratch):
    scratch = list(scratch)

    def take(n):
        got = scratch[:n]
        del scratch[:n]
        return got

    ag, snd, rcv = ([take(3) for _ in SETS] for _ in range(3))
    yb, ids, pos, zpos, perm, wv, raw, hs, cws, cwr, col, sbs, sbr = take(13)
    s_ag, r_ag, s_id, r_id, s_mv, r_mv, s_cw, r_cw, s_sb, r_sb, l_w, l_hs, l_out, l_own = take(14)

    ctx, tp = lax.axis_index("ctx"), lax.axis_index("tp")
    z, y, x, c = (ctx // 4) * 2 + tp // 8, ctx % 4, (tp // 2) % 4, tp % 2
    me = ctx * 16 + tp
    at = (z, y, x)
    slot = (y * 8 + x * 2 + c, z * 8 + x * 2 + c, y * 8 + z * 2 + c)

    def mate(p, d, core):
        return place(*(((v + d) % 4 if q == p else v) for q, v in enumerate(at)), core)

    barrier = pltpu.get_barrier_semaphore()
    for d in (1, 3, 2):
        for p in AXES:
            for core in (c, 1 - c):
                pl.semaphore_signal(barrier, inc=1, device_id=mate(p, d, core), device_id_type=MESH)
    pl.semaphore_signal(barrier, inc=1, device_id=place(z, y, x, 1 - c), device_id_type=MESH)

    own = []
    for s in SETS:
        for p in AXES:
            cols = pl.ds(starts[s][p], 2 * halves[s][p])
            own.append(pltpu.make_async_copy(grad_ref.at[:, cols], ag[s][p].at[at[p]], l_own.at[s * 3 + p]))
            own[-1].start()
    load_w = pltpu.make_async_copy(weight_ref.at[0], wv, l_w)
    load_hs = pltpu.make_async_copy(saved_ref.at[0], hs, l_hs)

    ids_t = ids_ref[...].astype(F32)
    scale_t = scale_ref[...].astype(F32)
    for p in AXES:
        ids[p * 4 + at[p], :8, :] = ids_t
        ids[p * 4 + at[p], 8:, :] = scale_t
    for copy in own:
        copy.wait()
    pl.semaphore_wait(barrier, 19)

    def gather(s, p, d):
        here = ag[s][p].at[at[p]]
        return pltpu.make_async_remote_copy(
            here, here, s_ag.at[s * 3 + p, d], r_ag.at[s * 3 + p, d], device_id=mate(p, d, c), device_id_type=MESH
        )

    def forward(s, p, d):
        half = ag[s][p].at[(at[p] + 4 - d) % 4, pl.ds(64 * (d // 2), 64)]
        return pltpu.make_async_remote_copy(
            half, half, s_ag.at[s * 3 + p, d - 1], r_ag.at[s * 3 + p, d - 1],
            device_id=mate(p, d, c), device_id_type=MESH,
        )

    def gather_ids(p, d):
        here = ids.at[p * 4 + at[p]]
        return pltpu.make_async_remote_copy(
            here, here, s_id, r_id, device_id=mate(p, d, c), device_id_type=MESH
        )

    for d in (1, 3, 2):
        for p in AXES:
            gather_ids(p, d).start()
    for s in SETS:
        for d in (1, 3):
            for p in AXES:
                gather(s, p, d).start()
    load_w.start()
    load_hs.start()

    before = jnp.where(iota((128, 128), 0) < iota((128, 128), 1), 1.0, 0.0).astype(BF16)
    expert = iota((128, 128), 0).astype(F32)

    def positions(table):
        named = jnp.zeros((128, 128), F32)
        for k in range(8):
            named = named + jnp.where(expert == table[k : k + 1, :], 1.0, 0.0)
        earlier = dot(named.astype(BF16), before)
        return jnp.where(named > 0.0, earlier, -1.0)

    nine = ids.at[pl.ds(0, 9)]
    pltpu.make_async_copy(nine, nine, r_id).wait()
    for p in AXES:
        for b in range(4):
            found = positions(ids[p * 4 + b])
            pos[p, :, b * 128 : (b + 1) * 128] = found.astype(BF16)
            if p == 0:
                zpos[b] = found

    lane8 = iota((8, 128), 1)

    def weigh(unit_y, _):
        first = pl.multiple_of(number(z, unit_y, 0, 0), 8)
        named = (iota((8, 128), 0) + first).astype(F32)
        rows = jnp.zeros((8, 128), F32)
        for b in range(4):
            scale = jnp.zeros((8, 128), F32)
            for k in range(8):
                scale = scale + jnp.where(named == ids[b, k : k + 1, :], ids[b, 8 + k : 9 + k, :], 0.0)
            which = zpos[b, pl.ds(first, 8), :]
            for j in range(CAP):
                column = jnp.sum(jnp.where(which == float(j), scale, 0.0), axis=1, keepdims=True)
                rows = rows + jnp.where(lane8 == b * CAP + j, column, 0.0)
        for g in range(8):
            cws[unit_y * 8 + g] = rows[g : g + 1]
        return 0

    def prepare():
        for q in range(2):
            row = iota((640, 1), 0)
            chunk, b, g, j = div(row, 320), rem(div(row, 80), 4), rem(div(row, 10), 8), rem(row, 10)
            if q == 0:
                source = g * 80 + chunk * 40 + b * 10 + j
            else:
                source = (b * 2 + rem(g, 2)) * 80 + chunk * 40 + div(g, 2) * 10 + j
            perm[q] = jnp.where(iota((640, 640), 1) == source, 1.0, 0.0).astype(BF16)
        raw[...] = jnp.zeros_like(raw)

    def relay(s):
        for d in (1, 3):
            for p in AXES:
                gather(s, p, d).wait_recv()
                forward(s, p, d).start()

    def arrived(s):
        for d in (1, 3):
            for p in AXES:
                forward(s, p, d).wait_recv()

    def target(p, k, g):
        d = (k + 1) % 4
        if p == 0:
            return (z, (y + d) % 4, g // 2, g % 2)
        if p == 1:
            return ((z + d) % 4, y, g // 2, g % 2)
        return (g // 2, (y + d) % 4, x, g % 2)

    def move(s, p, k, g):
        return pltpu.make_async_remote_copy(
            snd[s][p].at[k * 8 + g], rcv[s][p].at[slot[p]], s_mv.at[s, p * 4 + k],
            r_mv.at[s, p * 4 + slot[p] // 8],
            device_id=place(*target(p, k, g)), device_id_type=MESH,
        )

    def keep(s, p, g):
        return pltpu.make_async_copy(
            snd[s][p].at[24 + g], rcv[s][p].at[slot[p]], r_mv.at[s, p * 4 + slot[p] // 8]
        )

    def pick(s, k, p):
        row = iota((320, 1), 0)
        e, b, j = div(row, 40), rem(div(row, 10), 4), rem(row, 10)
        first = target(p, k, 0)
        if p == 2:
            who = number(div(e, 2), first[1], x, rem(e, 2))
        else:
            who = number(first[0], first[1], 0, 0) + e
        chosen = jnp.where(iota((320, 128), 1) == who, 1.0, 0.0).astype(BF16)
        value = dot(chosen, pos[p])
        hit = (value == j.astype(F32)) & (div(iota((1, 512), 1), 128) == b)
        onehot = jnp.where(hit, 1.0, 0.0).astype(BF16)
        h = halves[s][p]
        parts = [dot(onehot, ag[s][p][:, :, i * h : (i + 1) * h].reshape(512, h)) for i in range(2)]
        for g in range(8):
            both = [part[g * 40 : g * 40 + 40] for part in parts]
            snd[s][p][k * 8 + g] = jnp.concatenate(both, axis=0).astype(BF16)

    def send_stage(s, k, axes=AXES):
        for p in axes:
            pick(s, k, p)

        def send(i, _):
            for p in axes:
                own_g = (z if p == 2 else x) * 2 + c
                g = (((z if p == 2 else x) + i + 1 + k) % 4) * 2 + (c + i // 4) % 2
                itself = (k == 3) & (g == own_g)

                @pl.when(itself)
                def _():
                    keep(s, p, g).start()

                @pl.when(jnp.logical_not(itself))
                def _():
                    move(s, p, k, g).start()
            return 0

        lax.fori_loop(0, 8, send, 0)

    def sent(s, k):
        for p in AXES:
            eight, seven = snd[s][p].at[pl.ds(0, 8)], snd[s][p].at[pl.ds(0, 7)]

            @pl.when(k < 3)
            def _():
                pltpu.make_async_copy(eight, eight, s_mv.at[s, p * 4 + k]).wait()

            @pl.when(k == 3)
            def _():
                pltpu.make_async_copy(seven, seven, s_mv.at[s, p * 4 + k]).wait()

    def arrive(s, p, k):
        d = (k + 1) % 4
        block = ((y + 4 - d) % 4, (z + 4 - d) % 4, (y + 4 - d) % 4)[p]
        rows = rcv[s][p].at[pl.ds(block * 8, 8)]
        pltpu.make_async_copy(rows, rows, r_mv.at[s, p * 4 + block]).wait()
        h = halves[s][p]
        got = rcv[s][p][pl.ds(block * 8, 8)].reshape(640, h)
        ordered = dot(perm[1 if p == 2 else 0], got).astype(BF16)
        off = 2 * halves[s][0] if p == 2 else 0
        yb[:, off : off + h] = ordered[:320]
        yb[:, off + h : off + 2 * h] = ordered[320:]
        return block

    step = 512

    def terms(s, axes, out):
        start, width = starts[s][axes[0]], sum(2 * halves[s][p] for p in axes)
        return dot_t(yb[:, :width], wv[out, start : start + width])

    def column(unit_y, _):
        row = iota((80, 1), 0)
        spread = jnp.where(iota((80, 8), 1) == div(row, 10), 1.0, 0.0)
        weights = dot(spread.astype(BF16), cwr[pl.ds(unit_y * 8, 8)].reshape(8, 128).astype(BF16))
        for unit_z in range(4):
            mine = iota((80, 128), 1) == unit_z * CAP + rem(row, 10)
            weight = jnp.sum(jnp.where(mine, weights, 0.0), axis=1, keepdims=True)
            col[unit_y * 4 + unit_z] = jnp.broadcast_to(weight, (80, 128))
        return 0

    def finish(s, y_block):
        here = pl.ds(pl.multiple_of(y_block * 320, 320), 320)
        there = [pl.ds(pl.multiple_of((hi * 4 + y_block) * 160, 160), 160) for hi in range(2)]
        weight = col[pl.ds(y_block * 4, 4)].reshape(320, 128)[:, :1]
        summed = [jnp.zeros((160, 1), F32)] * 2
        for n in range(ff // step):
            out = slice(n * step, (n + 1) * step)
            total = raw[here, out] + terms(s, (0, 2), out)
            for hi in range(2):
                part = total[hi * 160 : (hi + 1) * 160]
                saved = hs[there[hi], out].astype(F32)
                summed[hi] = summed[hi] + jnp.sum(saved * part, axis=1, keepdims=True)
                hs[there[hi], out] = (weight[hi * 160 : (hi + 1) * 160] * part).astype(BF16)
        for hi in range(2):
            pltpu.make_async_copy(
                hs.at[there[hi]], out_ref.at[0, there[hi]], l_out.at[y_block * 2 + hi]
            ).start()
        j = rem(iota((320, 1), 0), 10)
        cells = jnp.where(iota((320, 128), 1) == j, jnp.concatenate(summed, axis=0), 0.0)
        group = jnp.where(iota((32, 320), 0) == div(iota((1, 320), 1), 10), 1.0, 0.0).astype(BF16)
        lines = jnp.zeros((32, 128), F32)
        for _ in range(3):
            piece = cells.astype(BF16)
            lines = lines + dot(group, piece)
            cells = cells - piece.astype(F32)
        for i in range(32):
            sbs[number(i // 8, y_block, 0, 0) + i % 8] = lines[i : i + 1]

        def give(i, _):
            who = number(i // 8, y_block, 0, 0) + i % 8

            @pl.when(who == me)
            def _():
                sbr[me] = sbs[me]

            @pl.when(who != me)
            def _():
                pltpu.make_async_remote_copy(
                    sbs.at[who], sbr.at[me], s_sb, r_sb,
                    device_id=place(i // 8, y_block, (i // 2) % 4, i % 2), device_id_type=MESH,
                ).start()

            return 0

        lax.fori_loop(0, 32, give, 0)

    def receive_zx(s, k):
        y_block = arrive(s, 0, k)
        arrive(s, 2, k)
        if s == SETS[-1]:
            finish(s, y_block)
            return
        here = pl.ds(pl.multiple_of(y_block * 320, 320), 320)

        def multiply(n, _):
            out = pl.ds(pl.multiple_of(n * step, step), step)
            raw[here, out] += terms(s, (0, 2), out)
            return 0

        lax.fori_loop(0, ff // step, multiply, 0)

    def receive_y(s, k):
        z_block = arrive(s, 1, k)

        def multiply(n, _):
            out = pl.ds(pl.multiple_of(n * step, step), step)
            acc = terms(s, (1,), out)
            for b in range(4):
                rows_b = pl.ds(pl.multiple_of(b * 320 + z_block * 80, 80), 80)
                raw[rows_b, out] += acc[b * 80 : (b + 1) * 80]
            return 0

        lax.fori_loop(0, ff // step, multiply, 0)

    def loop(lower, upper, *steps):
        def run(k, _):
            for do in steps:
                do(k)
            return 0

        lax.fori_loop(lower, upper, run, 0)

    def send_cw(i):
        unit_y, g = (y + i // 8) % 4, (x * 2 + c + i) % 8
        return pltpu.make_async_remote_copy(
            cws.at[unit_y * 8 + g], cwr.at[slot[0]], s_cw, r_cw,
            device_id=place(z, unit_y, g // 2, g % 2), device_id_type=MESH,
        )

    relay(0)
    stages = 4 * len(SETS)
    behind = 6

    def turn(t, _):
        for s in SETS:

            @pl.when(t == s * 4)
            def _():
                arrived(s)

            @pl.when(t // 4 == s)
            def _():
                if s < SETS[-1]:
                    send_stage(s, t % 4)
                else:
                    send_stage(s, t % 4)

            if s > 0:

                @pl.when(t == s - 1)
                def _():
                    relay(s)

        @pl.when(t == 1)
        def _():
            prepare()
            lax.fori_loop(0, 4, weigh, 0)
            loop(1, 32, lambda i: send_cw(i).start())
            cwr[slot[0]] = cws[slot[0]]
            load_w.wait()
            load_hs.wait()

        u = t - behind
        for s in SETS:
            if s == SETS[-1]:

                @pl.when(u == s * 4)
                def _():
                    pltpu.make_async_copy(all_cw, all_cw, r_cw).wait()
                    lax.fori_loop(0, 4, column, 0)

            @pl.when((u >= s * 4) & (u < s * 4 + 4))
            def _():
                k = u - s * 4
                sent(s, k)
                if s < SETS[-1]:
                    receive_zx(s, k)
                    receive_y(s, k)
                else:

                    @pl.when(k == 0)
                    def _():
                        loop(0, 4, lambda j: receive_y(s, j))

                    receive_zx(s, k)
        return 0

    all_cw = cwr.at[pl.ds(0, 31)]
    lax.fori_loop(0, stages + behind, turn, 0)

    all_sb = sbr.at[pl.ds(0, 127)]
    pltpu.make_async_copy(all_sb, all_sb, r_sb).wait()
    returned = sbr[...].reshape(128, 128)
    mine = zpos[z]
    found = jnp.zeros((128, 128), F32)
    for j in range(CAP):
        found = found + jnp.where(mine == float(j), returned[:, j : j + 1], 0.0)
    for k in range(8):
        chosen = jnp.where(expert == ids[z, k : k + 1, :], found, 0.0)
        comb_ref[k : k + 1, :] = jnp.sum(chosen, axis=0, keepdims=True)

    for s in SETS:
        for p in AXES:
            for d in (1, 3):
                gather(s, p, d).wait_send()
                forward(s, p, d).wait_send()
    pltpu.make_async_copy(nine, nine, s_id).wait()
    pltpu.make_async_copy(all_cw, all_cw, s_cw).wait()
    pltpu.make_async_copy(all_sb, all_sb, s_sb).wait()

    def stored(u):
        pltpu.make_async_copy(hs.at[pl.ds(0, 160)], out_ref.at[0, pl.ds(0, 160)], l_out.at[u]).wait()

    loop(0, 8, stored)


def per_device(out_grad, combine_weights, expert_ids, hidden_saved, down_weight):
    slots, ff = hidden_saved.shape[1:]
    halves = tuple(tuple(128 * n for n in share) for share in SHARES)
    starts, at = [], 0
    for s in SETS:
        starts.append([0, 0, 0])
        for p in (0, 2, 1):
            starts[s][p] = at
            at += 2 * halves[s][p]
    anywhere = pl.BlockSpec(memory_space=pl.ANY)
    vmem = pl.BlockSpec(memory_space=pltpu.VMEM)
    dma = pltpu.SemaphoreType.DMA
    flat = [h for s in SETS for h in halves[s]]

    def body(*refs):
        kernel(halves, starts, ff, *refs)

    hidden_grad, combine = pl.pallas_call(
        body,
        out_shape=(
            jax.ShapeDtypeStruct(hidden_saved.shape, BF16),
            jax.ShapeDtypeStruct((8, 128), F32),
        ),
        in_specs=[vmem, vmem, anywhere, anywhere, anywhere],
        out_specs=(anywhere, vmem),
        scratch_shapes=[pltpu.VMEM((4, 128, 2 * h), BF16) for h in flat]
        + [pltpu.VMEM((32, 80, h), BF16) for h in flat] * 2
        + [pltpu.VMEM((320, max(2 * (halves[s][0] + halves[s][2]) for s in SETS)), BF16)]
        + [
            pltpu.VMEM((12, 16, 128), F32),
            pltpu.VMEM((3, 128, 512), BF16),
            pltpu.VMEM((4, 128, 128), F32),
            pltpu.VMEM((2, 640, 640), BF16),
            pltpu.VMEM((ff, out_grad.shape[1]), BF16),
            pltpu.VMEM((slots, ff), F32),
            pltpu.VMEM((slots, ff), BF16),
            pltpu.VMEM((32, 1, 128), F32),
            pltpu.VMEM((32, 1, 128), F32),
            pltpu.VMEM((16, 80, 128), F32),
            pltpu.VMEM((128, 1, 128), F32),
            pltpu.VMEM((128, 1, 128), F32),
        ]
        + [dma((9, 4))] * 2
        + [dma] * 2
        + [dma((3, 12))] * 2
        + [dma] * 6
        + [dma((8,)), dma((9,))],
        compiler_params=pltpu.CompilerParams(
            collective_id=0, has_side_effects=True, vmem_limit_bytes=62 << 20
        ),
    )(expert_ids.T, combine_weights.T, out_grad, hidden_saved, down_weight)
    return hidden_grad, combine.T


def solution(mesh):
    both = ("ctx", "tp")
    in_specs = (P(both, None), P(both, None), P(both, None), P(both, None, None), P(both, None, None))
    out_specs = (P(both, None, None), P(both, None))
    return jax.shard_map(
        per_device, mesh=mesh, in_specs=in_specs, out_specs=out_specs, check_vma=False
    )
```

```python
import jax
import jax.numpy as jnp
from jax import lax
from jax.experimental import pallas as pl
from jax.experimental.pallas import tpu as pltpu
from jax.sharding import PartitionSpec as P

MESH = pl.DeviceIdType.MESH
F32 = jnp.float32
BF16 = jnp.bfloat16
CAP = 10
AXES = (0, 1, 2)
SETS = (0, 1, 2)
SHARES = ((2, 2, 2), (2, 2, 2), (1, 1, 2))


def place(z, y, x, c):
    return ((z // 2) * 4 + y, (z % 2) * 8 + x * 2 + c)


def number(z, y, x, c):
    return (z // 2) * 64 + y * 16 + (z % 2) * 8 + x * 2 + c


def iota(shape, dim):
    return lax.broadcasted_iota(jnp.int32, shape, dim)


def div(a, b):
    return lax.div(a, jnp.int32(b))


def rem(a, b):
    return lax.rem(a, jnp.int32(b))


def dot(a, b):
    return lax.dot_general(a, b, (((1,), (0,)), ((), ())), preferred_element_type=F32)


def dot_t(a, b):
    return lax.dot_general(a, b, (((1,), (1,)), ((), ())), preferred_element_type=F32)


def kernel(halves, starts, ff, ids_ref, scale_ref, grad_ref, saved_ref, weight_ref, out_ref, comb_ref, *scratch):
    scratch = list(scratch)

    def take(n):
        got = scratch[:n]
        del scratch[:n]
        return got

    ag, snd, rcv = ([take(3) for _ in SETS] for _ in range(3))
    yb, ids, pos, zpos, perm, wv, raw, hs, cws, cwr, col, sbs, sbr = take(13)
    s_ag, r_ag, s_id, r_id, s_mv, r_mv, s_cw, r_cw, s_sb, r_sb, l_w, l_hs, l_out, l_own = take(14)

    ctx, tp = lax.axis_index("ctx"), lax.axis_index("tp")
    z, y, x, c = (ctx // 4) * 2 + tp // 8, ctx % 4, (tp // 2) % 4, tp % 2
    me = ctx * 16 + tp
    at = (z, y, x)
    slot = (y * 8 + x * 2 + c, z * 8 + x * 2 + c, y * 8 + z * 2 + c)

    def mate(p, d, core):
        return place(*(((v + d) % 4 if q == p else v) for q, v in enumerate(at)), core)

    barrier = pltpu.get_barrier_semaphore()
    for d in (1, 3, 2):
        for p in AXES:
            for core in (c, 1 - c):
                pl.semaphore_signal(barrier, inc=1, device_id=mate(p, d, core), device_id_type=MESH)
    pl.semaphore_signal(barrier, inc=1, device_id=place(z, y, x, 1 - c), device_id_type=MESH)

    own = []
    for s in SETS:
        for p in AXES:
            cols = pl.ds(starts[s][p], 2 * halves[s][p])
            own.append(pltpu.make_async_copy(grad_ref.at[:, cols], ag[s][p].at[at[p]], l_own.at[s * 3 + p]))
            own[-1].start()
    load_w = pltpu.make_async_copy(weight_ref.at[0], wv, l_w)
    load_hs = pltpu.make_async_copy(saved_ref.at[0], hs, l_hs)

    ids_t = ids_ref[...].astype(F32)
    scale_t = scale_ref[...].astype(F32)
    for p in AXES:
        ids[p * 4 + at[p], :8, :] = ids_t
        ids[p * 4 + at[p], 8:, :] = scale_t
    for copy in own:
        copy.wait()
    pl.semaphore_wait(barrier, 19)

    def gather(s, p, d):
        here = ag[s][p].at[at[p]]
        return pltpu.make_async_remote_copy(
            here, here, s_ag.at[s * 3 + p, d], r_ag.at[s * 3 + p, d], device_id=mate(p, d, c), device_id_type=MESH
        )

    def forward(s, p, d):
        half = ag[s][p].at[(at[p] + 4 - d) % 4, pl.ds(64 * (d // 2), 64)]
        return pltpu.make_async_remote_copy(
            half, half, s_ag.at[s * 3 + p, d - 1], r_ag.at[s * 3 + p, d - 1],
            device_id=mate(p, d, c), device_id_type=MESH,
        )

    def gather_ids(p, d):
        here = ids.at[p * 4 + at[p]]
        return pltpu.make_async_remote_copy(
            here, here, s_id, r_id, device_id=mate(p, d, c), device_id_type=MESH
        )

    for d in (1, 3, 2):
        for p in AXES:
            gather_ids(p, d).start()
    for s in SETS:
        for d in (1, 3):
            for p in AXES:
                gather(s, p, d).start()
    load_w.start()
    load_hs.start()

    before = jnp.where(iota((128, 128), 0) < iota((128, 128), 1), 1.0, 0.0).astype(BF16)
    expert = iota((128, 128), 0).astype(F32)

    def positions(table):
        named = jnp.zeros((128, 128), F32)
        for k in range(8):
            named = named + jnp.where(expert == table[k : k + 1, :], 1.0, 0.0)
        earlier = dot(named.astype(BF16), before)
        return jnp.where(named > 0.0, earlier, -1.0)

    nine = ids.at[pl.ds(0, 9)]
    pltpu.make_async_copy(nine, nine, r_id).wait()
    for p in AXES:
        for b in range(4):
            found = positions(ids[p * 4 + b])
            pos[p, :, b * 128 : (b + 1) * 128] = found.astype(BF16)
            if p == 0:
                zpos[b] = found

    lane8 = iota((8, 128), 1)

    def weigh(unit_y, _):
        first = pl.multiple_of(number(z, unit_y, 0, 0), 8)
        named = (iota((8, 128), 0) + first).astype(F32)
        rows = jnp.zeros((8, 128), F32)
        for b in range(4):
            scale = jnp.zeros((8, 128), F32)
            for k in range(8):
                scale = scale + jnp.where(named == ids[b, k : k + 1, :], ids[b, 8 + k : 9 + k, :], 0.0)
            which = zpos[b, pl.ds(first, 8), :]
            for j in range(CAP):
                column = jnp.sum(jnp.where(which == float(j), scale, 0.0), axis=1, keepdims=True)
                rows = rows + jnp.where(lane8 == b * CAP + j, column, 0.0)
        for g in range(8):
            cws[unit_y * 8 + g] = rows[g : g + 1]
        return 0

    def prepare():
        for q in range(2):
            row = iota((640, 1), 0)
            chunk, b, g, j = div(row, 320), rem(div(row, 80), 4), rem(div(row, 10), 8), rem(row, 10)
            if q == 0:
                source = g * 80 + chunk * 40 + b * 10 + j
            else:
                source = (b * 2 + rem(g, 2)) * 80 + chunk * 40 + div(g, 2) * 10 + j
            perm[q] = jnp.where(iota((640, 640), 1) == source, 1.0, 0.0).astype(BF16)
        raw[...] = jnp.zeros_like(raw)

    def relay(s):
        for d in (1, 3):
            for p in AXES:
                gather(s, p, d).wait_recv()
                forward(s, p, d).start()

    def arrived(s):
        for d in (1, 3):
            for p in AXES:
                forward(s, p, d).wait_recv()

    def target(p, k, g):
        d = (k + 1) % 4
        if p == 0:
            return (z, (y + d) % 4, g // 2, g % 2)
        if p == 1:
            return ((z + d) % 4, y, g // 2, g % 2)
        return (g // 2, (y + d) % 4, x, g % 2)

    def move(s, p, k, g):
        return pltpu.make_async_remote_copy(
            snd[s][p].at[k * 8 + g], rcv[s][p].at[slot[p]], s_mv.at[s, p * 4 + k],
            r_mv.at[s, p * 4 + slot[p] // 8],
            device_id=place(*target(p, k, g)), device_id_type=MESH,
        )

    def keep(s, p, g):
        return pltpu.make_async_copy(
            snd[s][p].at[24 + g], rcv[s][p].at[slot[p]], r_mv.at[s, p * 4 + slot[p] // 8]
        )

    def pick(s, k, p):
        row = iota((320, 1), 0)
        e, b, j = div(row, 40), rem(div(row, 10), 4), rem(row, 10)
        first = target(p, k, 0)
        if p == 2:
            who = number(div(e, 2), first[1], x, rem(e, 2))
        else:
            who = number(first[0], first[1], 0, 0) + e
        chosen = jnp.where(iota((320, 128), 1) == who, 1.0, 0.0).astype(BF16)
        value = dot(chosen, pos[p])
        hit = (value == j.astype(F32)) & (div(iota((1, 512), 1), 128) == b)
        onehot = jnp.where(hit, 1.0, 0.0).astype(BF16)
        h = halves[s][p]
        parts = [dot(onehot, ag[s][p][:, :, i * h : (i + 1) * h].reshape(512, h)) for i in range(2)]
        for g in range(8):
            both = [part[g * 40 : g * 40 + 40] for part in parts]
            snd[s][p][k * 8 + g] = jnp.concatenate(both, axis=0).astype(BF16)

    def send_stage(s, k, axes=AXES):
        for p in axes:
            pick(s, k, p)

        def send(i, _):
            for p in axes:
                own_g = (z if p == 2 else x) * 2 + c
                g = (((z if p == 2 else x) + i + 1 + k) % 4) * 2 + (c + i // 4) % 2
                itself = (k == 3) & (g == own_g)

                @pl.when(itself)
                def _():
                    keep(s, p, g).start()

                @pl.when(jnp.logical_not(itself))
                def _():
                    move(s, p, k, g).start()
            return 0

        lax.fori_loop(0, 8, send, 0)

    def sent(s, k):
        for p in AXES:
            eight, seven = snd[s][p].at[pl.ds(0, 8)], snd[s][p].at[pl.ds(0, 7)]

            @pl.when(k < 3)
            def _():
                pltpu.make_async_copy(eight, eight, s_mv.at[s, p * 4 + k]).wait()

            @pl.when(k == 3)
            def _():
                pltpu.make_async_copy(seven, seven, s_mv.at[s, p * 4 + k]).wait()

    def arrive(s, p, k):
        d = (k + 1) % 4
        block = ((y + 4 - d) % 4, (z + 4 - d) % 4, (y + 4 - d) % 4)[p]
        rows = rcv[s][p].at[pl.ds(block * 8, 8)]
        pltpu.make_async_copy(rows, rows, r_mv.at[s, p * 4 + block]).wait()
        h = halves[s][p]
        got = rcv[s][p][pl.ds(block * 8, 8)].reshape(640, h)
        ordered = dot(perm[1 if p == 2 else 0], got).astype(BF16)
        off = 2 * halves[s][0] if p == 2 else 0
        yb[:, off : off + h] = ordered[:320]
        yb[:, off + h : off + 2 * h] = ordered[320:]
        return block

    step = 768

    def terms(s, axes, out):
        start, width = starts[s][axes[0]], sum(2 * halves[s][p] for p in axes)
        return dot_t(yb[:, :width], wv[out, start : start + width])

    def column(unit_y, _):
        row = iota((80, 1), 0)
        spread = jnp.where(iota((80, 8), 1) == div(row, 10), 1.0, 0.0)
        weights = dot(spread.astype(BF16), cwr[pl.ds(unit_y * 8, 8)].reshape(8, 128).astype(BF16))
        for unit_z in range(4):
            mine = iota((80, 128), 1) == unit_z * CAP + rem(row, 10)
            weight = jnp.sum(jnp.where(mine, weights, 0.0), axis=1, keepdims=True)
            col[unit_y * 4 + unit_z] = jnp.broadcast_to(weight, (80, 128))
        return 0

    def finish(s, y_block):
        here = pl.ds(pl.multiple_of(y_block * 320, 320), 320)
        there = [pl.ds(pl.multiple_of((hi * 4 + y_block) * 160, 160), 160) for hi in range(2)]
        weight = col[pl.ds(y_block * 4, 4)].reshape(320, 128)[:, :1]
        summed = [jnp.zeros((160, 1), F32)] * 2
        for n in range(ff // step):
            out = slice(n * step, (n + 1) * step)
            total = raw[here, out] + terms(s, (0, 2), out)
            for hi in range(2):
                part = total[hi * 160 : (hi + 1) * 160]
                saved = hs[there[hi], out].astype(F32)
                summed[hi] = summed[hi] + jnp.sum(saved * part, axis=1, keepdims=True)
                hs[there[hi], out] = (weight[hi * 160 : (hi + 1) * 160] * part).astype(BF16)
        for hi in range(2):
            pltpu.make_async_copy(
                hs.at[there[hi]], out_ref.at[0, there[hi]], l_out.at[y_block * 2 + hi]
            ).start()
        j = rem(iota((320, 1), 0), 10)
        cells = jnp.where(iota((320, 128), 1) == j, jnp.concatenate(summed, axis=0), 0.0)
        group = jnp.where(iota((32, 320), 0) == div(iota((1, 320), 1), 10), 1.0, 0.0).astype(BF16)
        lines = jnp.zeros((32, 128), F32)
        for _ in range(3):
            piece = cells.astype(BF16)
            lines = lines + dot(group, piece)
            cells = cells - piece.astype(F32)
        for i in range(32):
            sbs[number(i // 8, y_block, 0, 0) + i % 8] = lines[i : i + 1]

        def give(i, _):
            who = number(i // 8, y_block, 0, 0) + i % 8

            @pl.when(who == me)
            def _():
                sbr[me] = sbs[me]

            @pl.when(who != me)
            def _():
                pltpu.make_async_remote_copy(
                    sbs.at[who], sbr.at[me], s_sb, r_sb,
                    device_id=place(i // 8, y_block, (i // 2) % 4, i % 2), device_id_type=MESH,
                ).start()

            return 0

        lax.fori_loop(0, 32, give, 0)

    def receive_zx(s, k):
        y_block = arrive(s, 0, k)
        arrive(s, 2, k)
        if s == SETS[-1]:
            finish(s, y_block)
            return
        here = pl.ds(pl.multiple_of(y_block * 320, 320), 320)

        def multiply(n, _):
            out = pl.ds(pl.multiple_of(n * step, step), step)
            raw[here, out] += terms(s, (0, 2), out)
            return 0

        lax.fori_loop(0, ff // step, multiply, 0)

    def receive_y(s, k):
        z_block = arrive(s, 1, k)

        def multiply(n, _):
            out = pl.ds(pl.multiple_of(n * step, step), step)
            acc = terms(s, (1,), out)
            for b in range(4):
                rows_b = pl.ds(pl.multiple_of(b * 320 + z_block * 80, 80), 80)
                raw[rows_b, out] += acc[b * 80 : (b + 1) * 80]
            return 0

        lax.fori_loop(0, ff // step, multiply, 0)

    def loop(lower, upper, *steps):
        def run(k, _):
            for do in steps:
                do(k)
            return 0

        lax.fori_loop(lower, upper, run, 0)

    def send_cw(i):
        unit_y, g = (y + i // 8) % 4, (x * 2 + c + i) % 8
        return pltpu.make_async_remote_copy(
            cws.at[unit_y * 8 + g], cwr.at[slot[0]], s_cw, r_cw,
            device_id=place(z, unit_y, g // 2, g % 2), device_id_type=MESH,
        )

    relay(0)
    stages = 4 * len(SETS)
    behind = 6

    def turn(t, _):
        for s in SETS:

            @pl.when(t == s * 4)
            def _():
                arrived(s)

            @pl.when(t // 4 == s)
            def _():
                if s < SETS[-1]:
                    send_stage(s, t % 4)
                else:
                    send_stage(s, t % 4)

            if s > 0:

                @pl.when(t == s - 1)
                def _():
                    relay(s)

        @pl.when(t == 1)
        def _():
            prepare()
            lax.fori_loop(0, 4, weigh, 0)
            loop(1, 32, lambda i: send_cw(i).start())
            cwr[slot[0]] = cws[slot[0]]
            load_w.wait()
            load_hs.wait()

        u = t - behind
        for s in SETS:
            if s == SETS[-1]:

                @pl.when(u == s * 4)
                def _():
                    pltpu.make_async_copy(all_cw, all_cw, r_cw).wait()
                    lax.fori_loop(0, 4, column, 0)

            @pl.when((u >= s * 4) & (u < s * 4 + 4))
            def _():
                k = u - s * 4
                sent(s, k)
                if s < SETS[-1]:
                    receive_zx(s, k)
                    receive_y(s, k)
                else:

                    @pl.when(k == 0)
                    def _():
                        loop(0, 4, lambda j: receive_y(s, j))

                    receive_zx(s, k)
        return 0

    all_cw = cwr.at[pl.ds(0, 31)]
    lax.fori_loop(0, stages + behind, turn, 0)

    all_sb = sbr.at[pl.ds(0, 127)]
    pltpu.make_async_copy(all_sb, all_sb, r_sb).wait()
    returned = sbr[...].reshape(128, 128)
    mine = zpos[z]
    found = jnp.zeros((128, 128), F32)
    for j in range(CAP):
        found = found + jnp.where(mine == float(j), returned[:, j : j + 1], 0.0)
    for k in range(8):
        chosen = jnp.where(expert == ids[z, k : k + 1, :], found, 0.0)
        comb_ref[k : k + 1, :] = jnp.sum(chosen, axis=0, keepdims=True)

    for s in SETS:
        for p in AXES:
            for d in (1, 3):
                gather(s, p, d).wait_send()
                forward(s, p, d).wait_send()
    pltpu.make_async_copy(nine, nine, s_id).wait()
    pltpu.make_async_copy(all_cw, all_cw, s_cw).wait()
    pltpu.make_async_copy(all_sb, all_sb, s_sb).wait()

    def stored(u):
        pltpu.make_async_copy(hs.at[pl.ds(0, 160)], out_ref.at[0, pl.ds(0, 160)], l_out.at[u]).wait()

    loop(0, 8, stored)


def per_device(out_grad, combine_weights, expert_ids, hidden_saved, down_weight):
    slots, ff = hidden_saved.shape[1:]
    halves = tuple(tuple(128 * n for n in share) for share in SHARES)
    starts, at = [], 0
    for s in SETS:
        starts.append([0, 0, 0])
        for p in (0, 2, 1):
            starts[s][p] = at
            at += 2 * halves[s][p]
    anywhere = pl.BlockSpec(memory_space=pl.ANY)
    vmem = pl.BlockSpec(memory_space=pltpu.VMEM)
    dma = pltpu.SemaphoreType.DMA
    flat = [h for s in SETS for h in halves[s]]

    def body(*refs):
        kernel(halves, starts, ff, *refs)

    hidden_grad, combine = pl.pallas_call(
        body,
        out_shape=(
            jax.ShapeDtypeStruct(hidden_saved.shape, BF16),
            jax.ShapeDtypeStruct((8, 128), F32),
        ),
        in_specs=[vmem, vmem, anywhere, anywhere, anywhere],
        out_specs=(anywhere, vmem),
        scratch_shapes=[pltpu.VMEM((4, 128, 2 * h), BF16) for h in flat]
        + [pltpu.VMEM((32, 80, h), BF16) for h in flat] * 2
        + [pltpu.VMEM((320, max(2 * (halves[s][0] + halves[s][2]) for s in SETS)), BF16)]
        + [
            pltpu.VMEM((12, 16, 128), F32),
            pltpu.VMEM((3, 128, 512), BF16),
            pltpu.VMEM((4, 128, 128), F32),
            pltpu.VMEM((2, 640, 640), BF16),
            pltpu.VMEM((ff, out_grad.shape[1]), BF16),
            pltpu.VMEM((slots, ff), F32),
            pltpu.VMEM((slots, ff), BF16),
            pltpu.VMEM((32, 1, 128), F32),
            pltpu.VMEM((32, 1, 128), F32),
            pltpu.VMEM((16, 80, 128), F32),
            pltpu.VMEM((128, 1, 128), F32),
            pltpu.VMEM((128, 1, 128), F32),
        ]
        + [dma((9, 4))] * 2
        + [dma] * 2
        + [dma((3, 12))] * 2
        + [dma] * 6
        + [dma((8,)), dma((9,))],
        compiler_params=pltpu.CompilerParams(
            collective_id=0, has_side_effects=True, vmem_limit_bytes=62 << 20
        ),
    )(expert_ids.T, combine_weights.T, out_grad, hidden_saved, down_weight)
    return hidden_grad, combine.T


def solution(mesh):
    both = ("ctx", "tp")
    in_specs = (P(both, None), P(both, None), P(both, None), P(both, None, None), P(both, None, None))
    out_specs = (P(both, None, None), P(both, None))
    return jax.shard_map(
        per_device, mesh=mesh, in_specs=in_specs, out_specs=out_specs, check_vma=False
    )
```
